128 devices in a mesh: ep: 32 (over y_lo, z, x), rep: 4 (over y_hi, core).
Axes of the slice: x: 4, y: 4 (y_hi: 2, y_lo: 2; y = y_hi * 2 + y_lo), z: 4, core: 2. Of those that a mesh axis runs over, the one named last changes fastest.
Arguments:
- tokens: bfloat16 [4096, 4096], P('ep'), may hold values from -6 to 6
- out_grad: bfloat16 [4096, 4096], P('ep'), may hold values from -6 to 6
- expert_ids: int32 [4096, 8], P('ep'), may hold values from 0 to 15, all different within a row
- route_weights: float32 [4096, 8], P('ep'), may hold values from 0.05 to 0.6
- gate_up_weight: bfloat16 [32, 2, 768, 2048], P('ep', None, 'rep'), may hold values from -0.09375 to 0.09375
- down_weight: bfloat16 [32, 768, 2048], P('ep', 'rep'), may hold values from -0.21875 to 0.21875
- gate_up_m: float32 [32, 2, 768, 2048], P('ep', None, 'rep'), may hold values from -6 to 6
- gate_up_v: float32 [32, 2, 768, 2048], P('ep', None, 'rep'), may hold values from 1 to 100
- down_m: float32 [32, 768, 2048], P('ep', 'rep'), may hold values from -6 to 6
- down_v: float32 [32, 768, 2048], P('ep', 'rep'), may hold values from 1 to 100
Outputs:
- token_grad: bfloat16 [4096, 4096], P('ep', 'rep')
- new_gate_up: bfloat16 [32, 2, 768, 2048], P('ep', None, 'rep')
- new_down: bfloat16 [32, 768, 2048], P('ep', 'rep')
- new_gate_up_m: float32 [32, 2, 768, 2048], P('ep', None, 'rep')
- new_gate_up_v: float32 [32, 2, 768, 2048], P('ep', None, 'rep')
- new_down_m: float32 [32, 768, 2048], P('ep', 'rep')
- new_down_v: float32 [32, 768, 2048], P('ep', 'rep')
The draws below stay inside these ranges and needn't reach their ends.
Inputs may be any that keep to these rules, and one draw needn't show every extreme that they name: `expert_ids`: each row names 8 different experts, and every expert is named by some row.
All inputs are finite; a program needn't handle non-finite values.
Results may differ from the reference program's by a relative error of at most 0.015.
Values may be sent and summed in bfloat16 or wider, within the bound.
No kernel may reach another device: no remote copies, remote signals or barrier semaphores. Data moves between devices by JAX's collectives and lax.ppermute only.
A program may use at most 192 MiB of HBM per device.

```python
import math
import jax
import jax.numpy as jnp
from jax import lax

D = 4096
FF = 768
TOK_EP = 128
TOKENS = 4096
EXPERTS = 16
TOP = 8
SLOT = 40
N_EP = 32
N_REP = 4


def shard_levels(stream_key, extent, split, smallest, high):
    level, own = 1.0, jax.random.fold_in(stream_key, 6)
    for dim, shards_of in split:
        steps = jnp.exp(jax.random.uniform(jax.random.fold_in(own, dim), (shards_of,), jnp.float32, smallest / len(split), high / len(split)))
        level = level * jnp.repeat(steps, extent[dim] // shards_of).reshape([-1 if axis == dim else 1 for axis in range(len(extent))])
    return level


def distinct(key, rows, number_of, top, lift):
    ranking = jax.random.permutation(jax.random.fold_in(key, 1), number_of)
    pull = ranking
    for power in range(3):
        pull = pull * pull // number_of
    pull = pull * lift // number_of
    lots = jax.random.randint(jax.random.fold_in(key, 2), (rows, number_of), 0, 4096) + pull
    holders = jax.random.permutation(jax.random.fold_in(key, 3), rows)[jnp.arange(number_of) % rows]
    lots = jnp.where(jnp.arange(rows)[:, None] == holders[None, :], 1 << 14, lots)
    priority = lots * number_of + jnp.arange(number_of)
    return lax.top_k(priority.astype(jnp.int32), top)[1].astype(jnp.int32)


def scatter_about(own_key, extent, width, reach, split=(), kind=jnp.bfloat16):
    gain = shard_levels(own_key, extent, split, -0.22, 0.18) if split else 1.0
    array = jax.random.normal(own_key, extent, jnp.float32) * width * gain
    return jnp.minimum(jnp.maximum(array, -reach), reach).astype(kind)


def setup_inputs(seed: int = 0) -> dict:
    keys = jax.random.split(jax.random.key(seed), 11)
    tokens = scatter_about(keys[0], (TOKENS, D), 1.0, 6.0, ((0, 32),))
    out_grad = scatter_about(keys[1], (TOKENS, D), 1.0, 6.0, ((0, 32),))
    expert_ids = distinct(keys[2], TOKENS, EXPERTS, TOP, 8192)
    route_weights = jnp.clip(jnp.exp(math.log(0.6) - 2.4849067 * jax.random.uniform(keys[3], (TOKENS, TOP), jnp.float32) ** shard_levels(keys[3], (TOKENS, TOP), ((0, 32),), -0.2, 0.2)), 0.05, 0.6)
    gate_up_weight = scatter_about(keys[4], (2 * EXPERTS, 2, FF, D // 2), D ** -0.5, 0.09375, ((0, 32), (2, 4)))
    down_weight = scatter_about(keys[5], (2 * EXPERTS, FF, D // 2), FF ** -0.5, 0.21875, ((0, 32), (1, 4)))
    gate_up_m = scatter_about(keys[6], (2 * EXPERTS, 2, FF, D // 2), 1.0, 6.0, ((0, 32), (2, 4)), jnp.float32)
    gate_up_v = jnp.clip(jnp.exp(math.log(100.0) - 4.6051702 * jax.random.uniform(keys[7], (2 * EXPERTS, 2, FF, D // 2), jnp.float32) ** shard_levels(keys[7], (2 * EXPERTS, 2, FF, D // 2), ((0, 32), (2, 4)), -0.2, 0.2)), 1.0, 100.0)
    down_m = scatter_about(keys[8], (2 * EXPERTS, FF, D // 2), 1.0, 6.0, ((0, 32), (1, 4)), jnp.float32)
    down_v = jnp.clip(jnp.exp(math.log(100.0) - 4.6051702 * jax.random.uniform(keys[9], (2 * EXPERTS, FF, D // 2), jnp.float32) ** shard_levels(keys[9], (2 * EXPERTS, FF, D // 2), ((0, 32), (1, 4)), -0.2, 0.2)), 1.0, 100.0)
    return {"tokens": tokens, "out_grad": out_grad, "expert_ids": expert_ids, "route_weights": route_weights, "gate_up_weight": gate_up_weight, "down_weight": down_weight, "gate_up_m": gate_up_m, "gate_up_v": gate_up_v, "down_m": down_m, "down_v": down_v}


beta_first = 0.9
beta_second = 0.95
learn_rate = 0.01
decay_rate = 0.1
adam_epsilon = 1e-08
correct_first = 0.9999734386011124
correct_second = 0.994079470779666

def contract(left, right, left_dim, right_dim):
    return lax.dot_general(left, right, (((left_dim,), (right_dim,)), ((), ())), preferred_element_type=jnp.float32)

def adam_step(weight, first, second, grad):
    first_new = beta_first * first + (1.0 - beta_first) * grad
    second_new = beta_second * second + (1.0 - beta_second) * grad * grad
    wide = weight.astype(jnp.float32)
    update = first_new / correct_first / (jnp.sqrt(second_new / correct_second) + adam_epsilon)
    return ((wide - learn_rate * (update + decay_rate * wide)).astype(jnp.bfloat16), first_new, second_new)

def reference(tokens, out_grad, expert_ids, route_weights, gate_up_weight, down_weight, gate_up_m, gate_up_v, down_m, down_v):
    block_ids = expert_ids.reshape(N_EP, TOK_EP * TOP)
    onehot = (block_ids[:, :, None] == jnp.arange(EXPERTS, dtype=jnp.int32)[None, None, :]).astype(jnp.int32)
    ranks = lax.optimization_barrier(jnp.sum((jnp.cumsum(onehot, axis=1) - onehot) * onehot, axis=2)).reshape(TOKENS, TOP)
    kept = ranks < 2 * SLOT
    coeff = jnp.where(kept, route_weights, jnp.float32(0.0))
    gate_up_full = gate_up_weight.reshape(EXPERTS, 2, 2, FF, D // 2).transpose(0, 2, 1, 4, 3).reshape(EXPERTS, 2, D, FF)
    down_full = down_weight.reshape(EXPERTS, 2, FF, D // 2).transpose(0, 2, 1, 3).reshape(EXPERTS, FF, D)
    quarter = FF // N_REP
    capacity = N_EP * 2 * SLOT

    def per_expert(total, inputs):
        expert, weights_gu, weights_down = inputs
        named = (expert_ids == expert) & kept
        present = jnp.any(named, axis=1)
        scale = lax.optimization_barrier(jnp.sum(jnp.where(named, coeff, jnp.float32(0.0)), axis=1))
        order = jnp.argsort(jnp.where(present, 0, 1).astype(jnp.int32), stable=True)[:capacity].astype(jnp.int32)
        live = present[order]
        row_x = jnp.where(live[:, None], tokens[order], jnp.zeros((), jnp.bfloat16))
        row_dy = (scale[order][:, None] * out_grad[order].astype(jnp.float32)).astype(jnp.bfloat16)
        w_gate = weights_gu[0]
        w_up = weights_gu[1]
        gate = jnp.dot(row_x, w_gate, preferred_element_type=jnp.float32)
        up = jnp.dot(row_x, w_up, preferred_element_type=jnp.float32)
        sigma = jax.nn.sigmoid(gate)
        active = gate * sigma
        hidden = (active * up).astype(jnp.bfloat16)
        hidden_grad = contract(row_dy, weights_down, 1, 1)
        up_grad = (hidden_grad * active).astype(jnp.bfloat16)
        gate_grad = (hidden_grad * up * sigma * (1.0 + gate * (1.0 - sigma))).astype(jnp.bfloat16)
        grad_down = contract(hidden, row_dy, 0, 0)
        grad_gate = contract(row_x, gate_grad, 0, 0)
        grad_up = contract(row_x, up_grad, 0, 0)
        route_grad = jnp.zeros((capacity, D), jnp.float32)
        for index in range(N_REP):
            low = index * quarter
            high = low + quarter
            piece = contract(gate_grad[:, low:high], w_gate[:, low:high], 1, 1) + contract(up_grad[:, low:high], w_up[:, low:high], 1, 1)
            rounded = lax.optimization_barrier(piece.astype(jnp.bfloat16))
            route_grad = route_grad + rounded.astype(jnp.float32)
        total = total.at[order].add(jnp.where(live[:, None], route_grad, jnp.float32(0.0)))
        return (total, (jnp.stack([grad_gate, grad_up]), grad_down))
    start = jnp.zeros((TOKENS, D), jnp.float32)
    total, (grads_gu, grads_down) = lax.scan(per_expert, start, (jnp.arange(EXPERTS, dtype=jnp.int32), gate_up_full, down_full))
    grad_gu = grads_gu.reshape(EXPERTS, 2, 2, D // 2, FF).transpose(0, 2, 1, 4, 3).reshape(2 * EXPERTS, 2, FF, D // 2)
    grad_dn = grads_down.reshape(EXPERTS, FF, 2, D // 2).transpose(0, 2, 1, 3).reshape(2 * EXPERTS, FF, D // 2)
    new_gu, gu_first, gu_second = adam_step(gate_up_weight, gate_up_m, gate_up_v, grad_gu)
    new_dn, dn_first, dn_second = adam_step(down_weight, down_m, down_v, grad_dn)
    return (total.astype(jnp.bfloat16), new_gu, new_dn, gu_first, gu_second, dn_first, dn_second)
```

```python
import functools

import jax
import jax.numpy as jnp
from jax import lax
from jax.experimental import pallas as pl
from jax.experimental.pallas import tpu as pltpu
from jax.sharding import PartitionSpec as P

beta_first = 0.9
beta_second = 0.95
learn_rate = 0.01
decay_rate = 0.1
adam_epsilon = 1e-08
correct_first = 0.9999734386011124
correct_second = 0.994079470779666

N_EP = 32
EXPERTS = 16
TOK = 128
TOP = 8
HALF_ROWS = 40
ROWS = N_EP * HALF_ROWS
QUARTER = 1024
HALF = 2048
HID = 192
F32 = jnp.float32
BF16 = jnp.bfloat16


def from_partner(value, axis, mask):
    pairs = [(source, source ^ mask) for source in range(lax.axis_size(axis))]
    return lax.ppermute(value, axis, pairs)


def exchange_groups():
    groups = []
    for core in range(2):
        for plane in range(2):
            members = []
            for ep in range(N_EP):
                y_hi = plane ^ (ep // 16) if core == 1 else plane
                members.append(ep * 4 + y_hi * 2 + core)
            groups.append(members)
    return groups


def exchange(value):
    return lax.all_to_all(
        value.reshape(N_EP, HALF_ROWS, QUARTER),
        ("ep", "rep"),
        split_axis=0,
        concat_axis=0,
        tiled=True,
        axis_index_groups=exchange_groups(),
    ).reshape(ROWS, QUARTER)


def contract(left, right, left_dim, right_dim):
    return lax.dot_general(
        left, right, (((left_dim,), (right_dim,)), ((), ())), preferred_element_type=F32
    )


def adam_step(weight, first, second, grad):
    first_new = beta_first * first + (1.0 - beta_first) * grad
    second_new = beta_second * second + (1.0 - beta_second) * grad * grad
    wide = weight.astype(F32)
    update = first_new / correct_first / (jnp.sqrt(second_new / correct_second) + adam_epsilon)
    return (
        (wide - learn_rate * (update + decay_rate * wide)).astype(BF16),
        first_new,
        second_new,
    )


def slot_match(place, ids_t):
    y_lo, y_hi, core = place[0], place[1], place[2]
    expert = lax.broadcasted_iota(jnp.int32, (EXPERTS, TOK), 0)
    named = jnp.zeros((EXPERTS, TOK), jnp.int32)
    for k in range(TOP):
        named += jnp.where(ids_t[k : k + 1, :] == expert, 1, 0)
    earlier = (
        lax.broadcasted_iota(jnp.int32, (TOK, TOK), 0)
        < lax.broadcasted_iota(jnp.int32, (TOK, TOK), 1)
    ).astype(F32)
    rank = contract(named.astype(F32).astype(BF16), earlier.astype(BF16), 1, 0)
    code = jnp.where(named > 0, rank, -1.0).astype(BF16)
    row = lax.broadcasted_iota(jnp.int32, (ROWS, EXPERTS), 0)
    low = lax.broadcasted_iota(jnp.int32, (ROWS, EXPERTS), 1) * (2 * HALF_ROWS)
    spread = jnp.where((row >= low) & (row < low + 2 * HALF_ROWS), 1.0, 0.0).astype(BF16)
    code_row = contract(spread, code, 1, 0)
    line = lax.broadcasted_iota(jnp.int32, (ROWS, TOK), 0)
    block = (line * 1639) >> 16
    flip = jnp.where(core == 1, 1, 0)
    half = y_hi ^ (flip & (y_lo ^ (block >> 4)))
    wanted = line - block * HALF_ROWS + half * HALF_ROWS
    match = code_row == wanted.astype(F32)
    return match, block & 1, spread


def pick_matrix(match, holder):
    low = jnp.where(match & (holder == 0), 1.0, 0.0)
    high = jnp.where(match & (holder == 1), 1.0, 0.0)
    return jnp.concatenate([low, high], axis=1).astype(BF16)


def send_tokens_kernel(place, ids_ref, low_ref, high_ref, out_ref, pick_ref):
    match, holder, _ = slot_match(place, ids_ref[...])
    pick = pick_matrix(match, holder)
    pick_ref[...] = pick
    out_ref[...] = (
        contract(pick[:, :TOK], low_ref[...], 1, 0) + contract(pick[:, TOK:], high_ref[...], 1, 0)
    ).astype(BF16)


def send_grads_kernel(place, ids_ref, weight_ref, low_ref, high_ref, out_ref):
    ids = ids_ref[...]
    match, holder, spread = slot_match(place, ids)
    pick = pick_matrix(match, holder)
    expert = lax.broadcasted_iota(jnp.int32, (EXPERTS, TOK), 0)
    weight = weight_ref[...]
    coeff = jnp.zeros((EXPERTS, TOK), F32)
    for k in range(TOP):
        coeff += jnp.where(ids[k : k + 1, :] == expert, weight[k : k + 1, :], 0.0)
    first = coeff.astype(BF16)
    rest = coeff - first.astype(F32)
    second = rest.astype(BF16)
    third = (rest - second.astype(F32)).astype(BF16)
    wide = (contract(spread, first, 1, 0) + contract(spread, second, 1, 0)) + contract(
        spread, third, 1, 0
    )
    scale = jnp.sum(jnp.where(match, wide, 0.0), axis=1, keepdims=True)
    rows = contract(pick[:, :TOK], low_ref[...], 1, 0) + contract(
        pick[:, TOK:], high_ref[...], 1, 0
    )
    out_ref[...] = (scale * rows).astype(BF16)


def quarter_spec(first):
    return pl.BlockSpec((TOK, QUARTER), lambda i, place: (0, first + place[2]))


def send_tokens(place, ids_t, tokens):
    return pl.pallas_call(
        send_tokens_kernel,
        out_shape=(
            jax.ShapeDtypeStruct((ROWS, QUARTER), BF16),
            jax.ShapeDtypeStruct((ROWS, 2 * TOK), BF16),
        ),
        grid_spec=pltpu.PrefetchScalarGridSpec(
            num_scalar_prefetch=1,
            grid=(1,),
            in_specs=[
                pl.BlockSpec((TOP, TOK), lambda i, place: (0, 0)),
                quarter_spec(0),
                quarter_spec(2),
            ],
            out_specs=(
                pl.BlockSpec((ROWS, QUARTER), lambda i, place: (0, 0)),
                pl.BlockSpec((ROWS, 2 * TOK), lambda i, place: (0, 0)),
            ),
        ),
        compiler_params=pltpu.CompilerParams(vmem_limit_bytes=48 * 1024 * 1024),
        cost_estimate=pl.CostEstimate(
            flops=2 * ROWS * 256 * QUARTER, bytes_accessed=4_000_000, transcendentals=0
        ),
        name="send_tokens",
    )(place, ids_t, tokens, tokens)


def send_grads(place, ids_t, weight_t, out_grad):
    return pl.pallas_call(
        send_grads_kernel,
        out_shape=jax.ShapeDtypeStruct((ROWS, QUARTER), BF16),
        grid_spec=pltpu.PrefetchScalarGridSpec(
            num_scalar_prefetch=1,
            grid=(1,),
            in_specs=[
                pl.BlockSpec((TOP, TOK), lambda i, place: (0, 0)),
                pl.BlockSpec((TOP, TOK), lambda i, place: (0, 0)),
                quarter_spec(0),
                quarter_spec(2),
            ],
            out_specs=pl.BlockSpec((ROWS, QUARTER), lambda i, place: (0, 0)),
        ),
        compiler_params=pltpu.CompilerParams(vmem_limit_bytes=48 * 1024 * 1024),
        cost_estimate=pl.CostEstimate(
            flops=2 * ROWS * 256 * QUARTER, bytes_accessed=4_000_000, transcendentals=0
        ),
        name="send_grads",
    )(place, ids_t, weight_t, out_grad, out_grad)


def trade_halves(received, core):
    mine = lax.dynamic_slice(received, (core * (ROWS // 2), 0), (ROWS // 2, QUARTER))
    give = lax.dynamic_slice(received, ((1 - core) * (ROWS // 2), 0), (ROWS // 2, QUARTER))
    took = from_partner(give, "rep", 1)
    return jnp.where(
        core == 0,
        jnp.concatenate([mine, took], axis=1),
        jnp.concatenate([took, mine], axis=1),
    )


def per_device(
    tokens,
    out_grad,
    expert_ids,
    route_weights,
    gate_up_weight,
    down_weight,
    gate_up_m,
    gate_up_v,
    down_m,
    down_v,
):
    ep = lax.axis_index("ep")
    rep = lax.axis_index("rep")
    y_hi = rep // 2
    core = rep % 2
    place = jnp.stack([ep // 16, y_hi, core]).astype(jnp.int32)
    ids_t = expert_ids.T
    weight_t = route_weights.T

    own_gu, own_down = gate_up_weight[0], down_weight[0]
    y_gu, y_down = from_partner(own_gu, "rep", 2), from_partner(own_down, "rep", 2)
    core_gu, core_down = from_partner(own_gu, "rep", 1), from_partner(own_down, "rep", 1)
    far_gu, far_down = from_partner(y_gu, "rep", 1), from_partner(y_down, "rep", 1)

    send_x, pick = send_tokens(place, ids_t, tokens)
    row_x = trade_halves(exchange(send_x), core)
    send_dy = send_grads(place, ids_t, weight_t, out_grad)
    row_dy = trade_halves(exchange(send_dy), core)

    w_gu = jnp.stack([own_gu, core_gu, y_gu, far_gu]).reshape(8 * HID, HALF)
    w_down = jnp.stack([own_down, core_down, y_down, far_down]).reshape(4 * HID, HALF)

    rows = ROWS // 2
    part_gu = contract(w_gu, row_x, 1, 1).astype(BF16)
    full_gu = part_gu.astype(F32) + from_partner(part_gu, "ep", 1).astype(F32)
    full_gu = full_gu.reshape(4, 2, HID, rows)
    part_hg = contract(w_down, row_dy, 1, 1).astype(BF16)
    hidden_grad = part_hg.astype(F32) + from_partner(part_hg, "ep", 1).astype(F32)
    hidden_grad = hidden_grad.reshape(4, HID, rows)

    gate, up = full_gu[:, 0], full_gu[:, 1]
    sigma = jax.nn.sigmoid(gate)
    active = gate * sigma
    hidden = (active * up).astype(BF16).reshape(4 * HID, rows)
    grad_down = contract(hidden, row_dy, 1, 0).reshape(4, HID, HALF)
    up_grad = (hidden_grad * active).astype(BF16)
    gate_grad = (hidden_grad * up * sigma * (1.0 + gate * (1.0 - sigma))).astype(BF16)
    grad_both = jnp.stack([gate_grad, up_grad], axis=1).reshape(8 * HID, rows)

    piece = contract(grad_both, w_gu, 0, 0).astype(BF16)
    lower, upper = piece[:, :QUARTER], piece[:, QUARTER:]
    keep = jnp.where(core == 0, lower, upper)
    give = jnp.where(core == 0, upper, lower)
    took = from_partner(give, "rep", 1)
    back = exchange(
        jnp.where(
            core == 0,
            jnp.concatenate([keep, took], axis=0),
            jnp.concatenate([took, keep], axis=0),
        )
    )

    grad_gu = contract(grad_both, row_x, 1, 0).reshape(4, 2, HID, HALF)

    def reduce_rep(grad):
        took = from_partner(jnp.stack([grad[1], grad[3]]).astype(BF16), "rep", 1).astype(F32)
        here = grad[0] + took[0]
        there = (grad[2] + took[1]).astype(BF16)
        return here, there

    here_down, there_down = reduce_rep(grad_down)
    here_gu, there_gu = reduce_rep(grad_gu)
    total_down = (here_down + from_partner(there_down, "rep", 2).astype(F32))[None]
    total_gu = (here_gu + from_partner(there_gu, "rep", 2).astype(F32))[None]
    new_gu, gu_first, gu_second = adam_step(gate_up_weight, gate_up_m, gate_up_v, total_gu)
    new_down, down_first, down_second = adam_step(down_weight, down_m, down_v, total_down)

    token_sum = contract(pick, back, 0, 0)
    lower, upper = token_sum[:TOK], token_sum[TOK:]
    keep = jnp.where(y_hi == 0, lower, upper)
    give = jnp.where(y_hi == 0, upper, lower).astype(BF16)
    token_grad = (keep + from_partner(give, "rep", 2).astype(F32)).astype(BF16)
    return (token_grad, new_gu, new_down, gu_first, gu_second, down_first, down_second)


def solution(mesh):
    in_specs = (
        P("ep", None),
        P("ep", None),
        P("ep", None),
        P("ep", None),
        P("ep", None, "rep", None),
        P("ep", "rep", None),
        P("ep", None, "rep", None),
        P("ep", None, "rep", None),
        P("ep", "rep", None),
        P("ep", "rep", None),
    )
    out_specs = (
        P("ep", "rep"),
        P("ep", None, "rep", None),
        P("ep", "rep", None),
        P("ep", None, "rep", None),
        P("ep", None, "rep", None),
        P("ep", "rep", None),
        P("ep", "rep", None),
    )
    return jax.shard_map(
        per_device, mesh=mesh, in_specs=in_specs, out_specs=out_specs, check_vma=False
    )
```

```python
import functools

import jax
import jax.numpy as jnp
from jax import lax
from jax.experimental import pallas as pl
from jax.experimental.pallas import tpu as pltpu
from jax.sharding import PartitionSpec as P

beta_first = 0.9
beta_second = 0.95
learn_rate = 0.01
decay_rate = 0.1
adam_epsilon = 1e-08
correct_first = 0.9999734386011124
correct_second = 0.994079470779666

N_EP = 32
EXPERTS = 16
TOK = 128
TOP = 8
HALF_ROWS = 40
ROWS = N_EP * HALF_ROWS
QUARTER = 1024
HALF = 2048
HID = 192
F32 = jnp.float32
SCALE = 1_000_000
BF16 = jnp.bfloat16


SHORT = 0.03


def cost(micros):
    return pl.CostEstimate(flops=1, bytes_accessed=int(micros * SCALE), transcendentals=0)


def from_partner(value, axis, mask):
    pairs = [(source, source ^ mask) for source in range(lax.axis_size(axis))]
    return lax.ppermute(value, axis, pairs)


def exchange_groups():
    groups = []
    for core in range(2):
        for plane in range(2):
            members = []
            for step in range(N_EP):
                ep = (step + 16 * core) % N_EP
                y_hi = plane ^ (ep // 16) if core == 1 else plane
                members.append(ep * 4 + y_hi * 2 + core)
            groups.append(members)
    return groups


def exchange(value):
    return lax.all_to_all(
        value.reshape(N_EP, HALF_ROWS, QUARTER),
        ("ep", "rep"),
        split_axis=0,
        concat_axis=0,
        tiled=True,
        axis_index_groups=exchange_groups(),
    ).reshape(ROWS, QUARTER)


def contract(left, right, left_dim, right_dim):
    return lax.dot_general(
        left, right, (((left_dim,), (right_dim,)), ((), ())), preferred_element_type=F32
    )


def adam_step(weight, first, second, grad):
    first_new = beta_first * first + (1.0 - beta_first) * grad
    second_new = beta_second * second + (1.0 - beta_second) * grad * grad
    wide = weight.astype(F32)
    update = first_new / correct_first / (jnp.sqrt(second_new / correct_second) + adam_epsilon)
    return (
        (wide - learn_rate * (update + decay_rate * wide)).astype(BF16),
        first_new,
        second_new,
    )


def slot_match(place, ids_t):
    y_lo, y_hi, core = place[0], place[1], place[2]
    expert = lax.broadcasted_iota(jnp.int32, (EXPERTS, TOK), 0)
    named = jnp.zeros((EXPERTS, TOK), jnp.int32)
    for k in range(TOP):
        named += jnp.where(ids_t[k : k + 1, :] == expert, 1, 0)
    earlier = (
        lax.broadcasted_iota(jnp.int32, (TOK, TOK), 0)
        < lax.broadcasted_iota(jnp.int32, (TOK, TOK), 1)
    ).astype(F32)
    rank = contract(named.astype(F32).astype(BF16), earlier.astype(BF16), 1, 0)
    code = jnp.where(named > 0, rank, -1.0).astype(BF16)
    turn = core * (ROWS // 2)
    row = lax.broadcasted_iota(jnp.int32, (ROWS, EXPERTS), 0) + turn
    row = jnp.where(row >= ROWS, row - ROWS, row)
    low = lax.broadcasted_iota(jnp.int32, (ROWS, EXPERTS), 1) * (2 * HALF_ROWS)
    spread = jnp.where((row >= low) & (row < low + 2 * HALF_ROWS), 1.0, 0.0).astype(BF16)
    code_row = contract(spread, code, 1, 0)
    line = lax.broadcasted_iota(jnp.int32, (ROWS, TOK), 0) + turn
    line = jnp.where(line >= ROWS, line - ROWS, line)
    block = (line * 1639) >> 16
    flip = jnp.where(core == 1, 1, 0)
    half = y_hi ^ (flip & (y_lo ^ (block >> 4)))
    wanted = line - block * HALF_ROWS + half * HALF_ROWS
    match = code_row == wanted.astype(F32)
    return match, block & 1, spread


def pick_matrix(match, holder):
    low = jnp.where(match & (holder == 0), 1.0, 0.0)
    high = jnp.where(match & (holder == 1), 1.0, 0.0)
    return jnp.concatenate([low, high], axis=1).astype(BF16)


def send_tokens_kernel(place, ids_ref, low, high, out, pick_ref):
    match, holder, _ = slot_match(place, ids_ref[...])
    pick = pick_matrix(match, holder)
    pick_ref[...] = pick
    out[...] = (
        contract(pick[:, :TOK], low[...], 1, 0) + contract(pick[:, TOK:], high[...], 1, 0)
    ).astype(BF16)


def send_grads_kernel(place, ids_ref, weight_ref, pick_ref, low, high, out):
    ids = ids_ref[...]
    match, _, spread = slot_match(place, ids)
    expert = lax.broadcasted_iota(jnp.int32, (EXPERTS, TOK), 0)
    weight = weight_ref[...]
    coeff = jnp.zeros((EXPERTS, TOK), F32)
    for k in range(TOP):
        coeff += jnp.where(ids[k : k + 1, :] == expert, weight[k : k + 1, :], 0.0)
    first = coeff.astype(BF16)
    rest = coeff - first.astype(F32)
    second = rest.astype(BF16)
    third = (rest - second.astype(F32)).astype(BF16)
    wide = (contract(spread, first, 1, 0) + contract(spread, second, 1, 0)) + contract(
        spread, third, 1, 0
    )
    scale = jnp.sum(jnp.where(match, wide, 0.0), axis=1, keepdims=True)
    rows = contract(pick_ref[:, :TOK], low[...], 1, 0) + contract(
        pick_ref[:, TOK:], high[...], 1, 0
    )
    out[...] = (scale * rows).astype(BF16)


def quarter_spec(first):
    return pl.BlockSpec((TOK, QUARTER), lambda i, place: (0, first + place[2]))


def fixed_spec(shape):
    return pl.BlockSpec(shape, lambda i, place: (0, 0))


def send(kernel, place, small, wide, outs, name):
    specs = [fixed_spec(array.shape) for array in small]
    return pl.pallas_call(
        kernel,
        out_shape=tuple(jax.ShapeDtypeStruct(shape, BF16) for shape in outs),
        grid_spec=pltpu.PrefetchScalarGridSpec(
            num_scalar_prefetch=1,
            grid=(1,),
            in_specs=specs + [quarter_spec(0), quarter_spec(2)],
            out_specs=tuple(fixed_spec(shape) for shape in outs),
        ),
        compiler_params=pltpu.CompilerParams(vmem_limit_bytes=48 * 1024 * 1024),
        cost_estimate=cost(3),
        name=name,
    )(place, *small, wide, wide)


SUB = ROWS // 2
CHUNK = HID // 2
ANY = pl.BlockSpec(memory_space=pl.ANY)
WHOLE = pl.BlockSpec(memory_space=pltpu.VMEM)
SMEM = pl.BlockSpec(memory_space=pltpu.SMEM)
PARAMS = pltpu.CompilerParams(vmem_limit_bytes=56 * 1024 * 1024)


def columns(place, other):
    start = pl.multiple_of(jnp.where(other, 1 - place[2], place[2]) * QUARTER, QUARTER)
    return pl.ds(start, QUARTER)


def project_kernel(parts_per_out, place, own, took, *refs):
    count = sum(parts_per_out)
    parts, outs = refs[:count], refs[count : count + len(parts_per_out)]
    x_out, x, w, sems = refs[count + len(parts_per_out) :]
    size = parts[0].shape[0]
    copies = [
        pltpu.make_async_copy(
            own.at[pl.ds(0, SUB)], x.at[:, columns(place, False)], sems.at[0]
        ),
        pltpu.make_async_copy(took, x.at[:, columns(place, True)], sems.at[1]),
    ]
    for j, part in enumerate(parts):
        copies.append(
            pltpu.make_async_copy(part, w.at[pl.ds(j * size, size)], sems.at[3 + j])
        )
    for copy in copies:
        copy.start()
    copies[0].wait()
    copies[1].wait()
    store = pltpu.make_async_copy(x, x_out, sems.at[2])
    store.start()
    for copy in copies[2:]:
        copy.wait()
    row = 0
    for out, number in zip(outs, parts_per_out):
        out[...] = contract(w[row : row + number * size, :], x[...], 1, 1).astype(BF16)
        row += number * size
    store.wait()


def project(place, received, took, groups, name, micros):
    parts = [part for group in groups for part in group]
    size = parts[0].shape[0]
    counts = tuple(len(group) for group in groups)
    return pl.pallas_call(
        functools.partial(project_kernel, counts),
        out_shape=tuple(jax.ShapeDtypeStruct((size * n, SUB), BF16) for n in counts)
        + (jax.ShapeDtypeStruct((SUB, HALF), BF16),),
        in_specs=[SMEM] + [ANY] * (2 + len(parts)),
        out_specs=(WHOLE,) * len(counts) + (ANY,),
        scratch_shapes=[
            pltpu.VMEM((SUB, HALF), BF16),
            pltpu.VMEM((len(parts) * size, HALF), BF16),
            pltpu.SemaphoreType.DMA((3 + len(parts),)),
        ],
        compiler_params=PARAMS,
        cost_estimate=cost(micros),
        name=name,
    )(place, received, took, *parts)


def block(shape, row=0):
    return pl.BlockSpec(shape, lambda i: (row, 0))


def single(kernel, outs, ins, micros, name):
    return pl.pallas_call(
        kernel,
        grid=(1,),
        out_shape=tuple(jax.ShapeDtypeStruct(shape, kind) for shape, kind in outs),
        in_specs=[block(shape, row) for _, shape, row in ins],
        out_specs=tuple(block(shape) for shape, _ in outs),
        compiler_params=PARAMS,
        cost_estimate=cost(micros),
        name=name,
    )(*[array for array, _, _ in ins])


def full(array):
    return array, array.shape, 0


def hidden_kernel(ours, theirs, dy, active_out, slope_out, hidden_here, *grad_away):
    hidden = [None] * 4
    for j in range(4):
        gate_rows, up_rows = pl.ds(2 * j * HID, HID), pl.ds((2 * j + 1) * HID, HID)
        gate = ours[gate_rows, :].astype(F32) + theirs[gate_rows, :].astype(F32)
        up = ours[up_rows, :].astype(F32) + theirs[up_rows, :].astype(F32)
        sigma = jax.nn.sigmoid(gate)
        active = gate * sigma
        rows = pl.ds(j * HID, HID)
        active_out[rows, :] = active
        slope_out[rows, :] = up * sigma * (1.0 + gate * (1.0 - sigma))
        hidden[j] = (active * up).astype(BF16)
    hidden_here[:HID, :] = hidden[0]
    hidden_here[HID:, :] = hidden[1]
    total = contract(jnp.concatenate(hidden[2:], axis=0), dy[...], 1, 0).astype(BF16)
    for j, out in enumerate(grad_away):
        out[...] = total[j * CHUNK : (j + 1) * CHUNK]


def here_kernel(rows, x, add, mine, there):
    size = mine.shape[0]
    mine[...] = contract(rows[:size, :], x[...], 1, 0) + add[:size, :].astype(F32)
    there[...] = (contract(rows[size:, :], x[...], 1, 0) + add[size:, :].astype(F32)).astype(BF16)


def down_here_kernel(rows, x, add0, add1, add2, add3, mine, there):
    mine[...] = contract(rows[:HID, :], x[...], 1, 0)
    mine[:CHUNK, :] += add0[...].astype(F32)
    mine[CHUNK:, :] += add1[...].astype(F32)
    total = contract(rows[HID:, :], x[...], 1, 0)
    there[:CHUNK, :] = (total[:CHUNK] + add2[...].astype(F32)).astype(BF16)
    there[CHUNK:, :] = (total[CHUNK:] + add3[...].astype(F32)).astype(BF16)


def grad_here(rows, x, add, micros, name):
    size = rows.shape[0] // 2
    outs = [((size, HALF), F32), ((size, HALF), BF16)]
    return single(here_kernel, outs, [full(rows), full(x), full(add)], micros, name)


def away_kernel(rows, x, out):
    out[...] = contract(rows[...], x[...], 1, 0).astype(BF16)


def piece_kernel(
    place, ours, theirs, active, slope, part0, part1, part2, part3, here, away, keep, give0, give1, w, sems
):
    copies = []
    for j, part in enumerate((part0, part1, part2, part3)):
        copies.append(
            pltpu.make_async_copy(part, w.at[pl.ds(2 * j * HID, 2 * HID)], sems.at[j])
        )
    for copy in copies:
        copy.start()
    for out, low in ((here, 0), (away, 2)):
        for j in range(2):
            rows = pl.ds((low + j) * HID, HID)
            grad = ours[rows, :].astype(F32) + theirs[rows, :].astype(F32)
            out[pl.ds(2 * j * HID, HID), :] = (grad * slope[rows, :]).astype(BF16)
            out[pl.ds((2 * j + 1) * HID, HID), :] = (grad * active[rows, :]).astype(BF16)
    both = jnp.concatenate([here[...], away[...]], axis=0)
    for copy in copies:
        copy.wait()
    total = contract(both, w[:, columns(place, True)], 0, 0).astype(BF16)
    give0[...] = total[: SUB // 2]
    give1[...] = total[SUB // 2 :]
    keep[...] = contract(both, w[:, columns(place, False)], 0, 0).astype(BF16)


def pieces(place, ours, theirs, active, slope, parts, micros):
    outs = [(4 * HID, SUB)] * 2 + [(ROWS, QUARTER)] + [(SUB // 2, QUARTER)] * 2
    blocks = [(4 * HID, SUB)] * 2 + [(SUB, QUARTER)] + [(SUB // 2, QUARTER)] * 2
    return pl.pallas_call(
        piece_kernel,
        grid=(1,),
        out_shape=tuple(jax.ShapeDtypeStruct(shape, BF16) for shape in outs),
        in_specs=[SMEM] + [block((4 * HID, SUB))] * 4 + [ANY] * 4,
        out_specs=tuple(block(shape) for shape in blocks),
        scratch_shapes=[
            pltpu.VMEM((8 * HID, HALF), BF16),
            pltpu.SemaphoreType.DMA((4,)),
        ],
        compiler_params=PARAMS,
        cost_estimate=cost(micros),
        name="pieces",
    )(place, ours, theirs, active, slope, *parts)


def adam_kernel(weight, first, second, mine, took, new_weight, new_first, new_second):
    grad = mine[...] + took[...].astype(F32)
    new_weight[...], new_first[...], new_second[...] = adam_step(
        weight[...], first[...], second[...], grad
    )


def adam(weight, first, second, mine, took, micros, name):
    rows = mine.shape[0]
    step = 32
    spec = pl.BlockSpec((step, HALF), lambda i: (i, 0))
    flat = (rows, HALF)
    outs = pl.pallas_call(
        adam_kernel,
        grid=(rows // step,),
        out_shape=(
            jax.ShapeDtypeStruct(flat, BF16),
            jax.ShapeDtypeStruct(flat, F32),
            jax.ShapeDtypeStruct(flat, F32),
        ),
        in_specs=[spec] * 5,
        out_specs=(spec,) * 3,
        compiler_params=pltpu.CompilerParams(vmem_limit_bytes=16 * 1024 * 1024),
        cost_estimate=cost(micros),
        name=name,
    )(weight.reshape(flat), first.reshape(flat), second.reshape(flat), mine, took)
    return [out.reshape(weight.shape) for out in outs]


def per_device(
    tokens,
    out_grad,
    expert_ids,
    route_weights,
    gate_up_weight,
    down_weight,
    gate_up_m,
    gate_up_v,
    down_m,
    down_v,
):
    ep = lax.axis_index("ep")
    rep = lax.axis_index("rep")
    y_hi = rep // 2
    core = rep % 2
    place = jnp.stack([ep // 16, y_hi, core]).astype(jnp.int32)
    ids_t = expert_ids.T
    weight_t = route_weights.T

    own_gu, own_down = gate_up_weight.reshape(2 * HID, HALF), down_weight.reshape(HID, HALF)
    y_gu, y_down = from_partner(own_gu, "rep", 2), from_partner(own_down, "rep", 2)
    core_gu, core_down = from_partner(own_gu, "rep", 1), from_partner(own_down, "rep", 1)
    far_gu, far_down = from_partner(y_gu, "rep", 1), from_partner(y_down, "rep", 1)

    send_x, pick = send(
        send_tokens_kernel, place, [ids_t], tokens, [(ROWS, QUARTER), (ROWS, 2 * TOK)], "send_tokens"
    )
    got_x = exchange(send_x)
    took_x = from_partner(got_x[SUB:], "rep", 1)
    (send_dy,) = send(
        send_grads_kernel, place, [ids_t, weight_t, pick], out_grad, [(ROWS, QUARTER)], "send_grads"
    )
    send_dy, far_gu = lax.optimization_barrier((send_dy, far_gu))
    got_dy = exchange(send_dy)

    gu_parts = (own_gu, y_gu, core_gu, far_gu)
    part_gu, row_x = project(place, got_x, took_x, [gu_parts], "project_gate_up", 10)
    there_gu = from_partner(part_gu, "ep", 1)
    late_dy, _ = lax.optimization_barrier((got_dy, part_gu))
    took_dy = from_partner(late_dy[SUB:], "rep", 1)
    part_hg, row_dy = project(
        place, late_dy, took_dy, [(own_down, y_down, core_down, far_down)], "project_down", 7
    )
    there_hg = from_partner(part_hg, "ep", 1)

    half = (2 * HID, SUB)
    active, slope, hidden_here, *down_away = single(
        hidden_kernel,
        [((4 * HID, SUB), F32), ((4 * HID, SUB), F32), (half, BF16)]
        + [((CHUNK, HALF), BF16)] * 4,
        [full(part_gu), full(there_gu), full(row_dy)],
        SHORT,
        "hidden_and_down",
    )
    down_mine, down_send = single(
        down_here_kernel,
        [((HID, HALF), F32), ((HID, HALF), BF16)],
        [full(hidden_here), full(row_dy)]
        + [full(from_partner(chunk, "rep", 1)) for chunk in down_away],
        SHORT,
        "down_here",
    )
    active, slope, down_send = lax.optimization_barrier((active, slope, down_send))
    down_there = from_partner(down_send, "rep", 2)
    both_here, both_away, keep, *give = pieces(
        place, part_hg, there_hg, active, slope, gu_parts, SHORT
    )
    took_give = [from_partner(chunk, "rep", 1) for chunk in give]
    (away,) = single(
        away_kernel, [((4 * HID, HALF), BF16)], [full(both_away), full(row_x)], SHORT, "grad_away"
    )
    took_give, away, down_there = lax.optimization_barrier((took_give, away, down_there))
    for j, chunk in enumerate(took_give):
        keep = lax.dynamic_update_slice(keep, chunk, (SUB + j * SUB // 2, 0))
    back = exchange(keep)
    mine, there = grad_here(both_here, row_x, from_partner(away, "rep", 1), 7, "grad_here")
    gu_there = from_partner(there, "rep", 2)
    new_gu, gu_first, gu_second = adam(
        gate_up_weight, gate_up_m, gate_up_v, mine, gu_there, 8, "adam_gate_up"
    )
    new_down, down_first, down_second = adam(
        down_weight, down_m, down_v, down_mine, down_there, 4, "adam_down"
    )

    token_sum = contract(pick, back, 0, 0)
    lower, upper = token_sum[:TOK], token_sum[TOK:]
    keep_sum = jnp.where(y_hi == 0, lower, upper)
    give_sum = jnp.where(y_hi == 0, upper, lower).astype(BF16)
    took_sum, new_gu, new_down = lax.optimization_barrier(
        (from_partner(give_sum, "rep", 2), new_gu, new_down)
    )
    token_grad = (keep_sum + took_sum.astype(F32)).astype(BF16)
    return (token_grad, new_gu, new_down, gu_first, gu_second, down_first, down_second)


def solution(mesh):
    in_specs = (
        P("ep", None),
        P("ep", None),
        P("ep", None),
        P("ep", None),
        P("ep", None, "rep", None),
        P("ep", "rep", None),
        P("ep", None, "rep", None),
        P("ep", None, "rep", None),
        P("ep", "rep", None),
        P("ep", "rep", None),
    )
    out_specs = (
        P("ep", "rep"),
        P("ep", None, "rep", None),
        P("ep", "rep", None),
        P("ep", None, "rep", None),
        P("ep", None, "rep", None),
        P("ep", "rep", None),
        P("ep", "rep", None),
    )
    return jax.shard_map(
        per_device, mesh=mesh, in_specs=in_specs, out_specs=out_specs, check_vma=False
    )
```

```python
import functools

import jax
import jax.numpy as jnp
from jax import lax
from jax.experimental import pallas as pl
from jax.experimental.pallas import tpu as pltpu
from jax.sharding import PartitionSpec as P

beta_first = 0.9
beta_second = 0.95
learn_rate = 0.01
decay_rate = 0.1
adam_epsilon = 1e-08
correct_first = 0.9999734386011124
correct_second = 0.994079470779666

N_EP = 32
EXPERTS = 16
TOK = 128
TOP = 8
HALF_ROWS = 40
ROWS = N_EP * HALF_ROWS
QUARTER = 1024
HALF = 2048
HID = 192
F32 = jnp.float32
SCALE = 1_000_000
UPDATE = 5 * 10**12
BF16 = jnp.bfloat16


SHORT = 0.03


def cost(micros):
    return pl.CostEstimate(flops=1, bytes_accessed=int(micros * SCALE), transcendentals=0)


def from_partner(value, axis, mask):
    pairs = [(source, source ^ mask) for source in range(lax.axis_size(axis))]
    return lax.ppermute(value, axis, pairs)


def exchange_groups():
    groups = []
    for core in range(2):
        for plane in range(2):
            members = []
            for step in range(N_EP):
                ep = (step + 16 * core) % N_EP
                y_hi = plane ^ (ep // 16) if core == 1 else plane
                members.append(ep * 4 + y_hi * 2 + core)
            groups.append(members)
    return groups


def exchange(value):
    return lax.all_to_all(
        value.reshape(N_EP, HALF_ROWS, QUARTER),
        ("ep", "rep"),
        split_axis=0,
        concat_axis=0,
        tiled=True,
        axis_index_groups=exchange_groups(),
    ).reshape(ROWS, QUARTER)


def contract(left, right, left_dim, right_dim):
    return lax.dot_general(
        left, right, (((left_dim,), (right_dim,)), ((), ())), preferred_element_type=F32
    )


def adam_step(weight, first, second, grad):
    first_new = beta_first * first + (1.0 - beta_first) * grad
    second_new = beta_second * second + (1.0 - beta_second) * grad * grad
    wide = weight.astype(F32)
    update = first_new / correct_first / (jnp.sqrt(second_new / correct_second) + adam_epsilon)
    return (
        (wide - learn_rate * (update + decay_rate * wide)).astype(BF16),
        first_new,
        second_new,
    )


def slot_match(place, ids_t):
    y_lo, y_hi, core = place[0], place[1], place[2]
    expert = lax.broadcasted_iota(jnp.int32, (EXPERTS, TOK), 0)
    named = jnp.zeros((EXPERTS, TOK), jnp.int32)
    for k in range(TOP):
        named += jnp.where(ids_t[k : k + 1, :] == expert, 1, 0)
    earlier = (
        lax.broadcasted_iota(jnp.int32, (TOK, TOK), 0)
        < lax.broadcasted_iota(jnp.int32, (TOK, TOK), 1)
    ).astype(F32)
    rank = contract(named.astype(F32).astype(BF16), earlier.astype(BF16), 1, 0)
    code = jnp.where(named > 0, rank, -1.0).astype(BF16)
    turn = core * (ROWS // 2)
    row = lax.broadcasted_iota(jnp.int32, (ROWS, EXPERTS), 0) + turn
    row = jnp.where(row >= ROWS, row - ROWS, row)
    low = lax.broadcasted_iota(jnp.int32, (ROWS, EXPERTS), 1) * (2 * HALF_ROWS)
    spread = jnp.where((row >= low) & (row < low + 2 * HALF_ROWS), 1.0, 0.0).astype(BF16)
    code_row = contract(spread, code, 1, 0)
    line = lax.broadcasted_iota(jnp.int32, (ROWS, TOK), 0) + turn
    line = jnp.where(line >= ROWS, line - ROWS, line)
    block = (line * 1639) >> 16
    flip = jnp.where(core == 1, 1, 0)
    half = y_hi ^ (flip & (y_lo ^ (block >> 4)))
    wanted = line - block * HALF_ROWS + half * HALF_ROWS
    match = code_row == wanted.astype(F32)
    return match, block & 1, spread


def pick_matrix(match, holder):
    low = jnp.where(match & (holder == 0), 1.0, 0.0)
    high = jnp.where(match & (holder == 1), 1.0, 0.0)
    return jnp.concatenate([low, high], axis=1).astype(BF16)


def send_tokens_kernel(place, ids_ref, low, high, out, pick_ref):
    match, holder, _ = slot_match(place, ids_ref[...])
    pick = pick_matrix(match, holder)
    pick_ref[...] = pick
    out[...] = (
        contract(pick[:, :TOK], low[...], 1, 0) + contract(pick[:, TOK:], high[...], 1, 0)
    ).astype(BF16)


def send_grads_kernel(place, ids_ref, weight_ref, pick_ref, low, high, out):
    ids = ids_ref[...]
    match, _, spread = slot_match(place, ids)
    expert = lax.broadcasted_iota(jnp.int32, (EXPERTS, TOK), 0)
    weight = weight_ref[...]
    coeff = jnp.zeros((EXPERTS, TOK), F32)
    for k in range(TOP):
        coeff += jnp.where(ids[k : k + 1, :] == expert, weight[k : k + 1, :], 0.0)
    first = coeff.astype(BF16)
    rest = coeff - first.astype(F32)
    second = rest.astype(BF16)
    third = (rest - second.astype(F32)).astype(BF16)
    wide = (contract(spread, first, 1, 0) + contract(spread, second, 1, 0)) + contract(
        spread, third, 1, 0
    )
    scale = jnp.sum(jnp.where(match, wide, 0.0), axis=1, keepdims=True)
    rows = contract(pick_ref[:, :TOK], low[...], 1, 0) + contract(
        pick_ref[:, TOK:], high[...], 1, 0
    )
    out[...] = (scale * rows).astype(BF16)


def quarter_spec(first):
    return pl.BlockSpec((TOK, QUARTER), lambda i, place: (0, first + place[2]))


def fixed_spec(shape):
    return pl.BlockSpec(shape, lambda i, place: (0, 0))


def send(kernel, place, small, wide, outs, name):
    specs = [fixed_spec(array.shape) for array in small]
    return pl.pallas_call(
        kernel,
        out_shape=tuple(jax.ShapeDtypeStruct(shape, BF16) for shape in outs),
        grid_spec=pltpu.PrefetchScalarGridSpec(
            num_scalar_prefetch=1,
            grid=(1,),
            in_specs=specs + [quarter_spec(0), quarter_spec(2)],
            out_specs=tuple(fixed_spec(shape) for shape in outs),
        ),
        compiler_params=pltpu.CompilerParams(vmem_limit_bytes=48 * 1024 * 1024),
        cost_estimate=cost(3),
        name=name,
    )(place, *small, wide, wide)


SUB = ROWS // 2
CHUNK = HID // 2
CUT = SUB // 2
ANY = pl.BlockSpec(memory_space=pl.ANY)
WHOLE = pl.BlockSpec(memory_space=pltpu.VMEM)
SMEM = pl.BlockSpec(memory_space=pltpu.SMEM)
PARAMS = pltpu.CompilerParams(vmem_limit_bytes=56 * 1024 * 1024)


def columns(place, other):
    start = pl.multiple_of(jnp.where(other, 1 - place[2], place[2]) * QUARTER, QUARTER)
    return pl.ds(start, QUARTER)


def project_kernel(chunks, place, own, *refs):
    took, refs = refs[:chunks], refs[chunks:]
    parts, (out, x_out, x, w, sems) = refs[:-5], refs[-5:]
    size, step = parts[0].shape[0], SUB // chunks
    loads = [
        pltpu.make_async_copy(own.at[pl.ds(0, SUB)], x.at[:, columns(place, False)], sems.at[0])
    ]
    for j, chunk in enumerate(took):
        target = x.at[pl.ds(j * step, step), columns(place, True)]
        loads.append(pltpu.make_async_copy(chunk, target, sems.at[2 + j]))
    for j, part in enumerate(parts):
        target = w.at[pl.ds(j * size, size)]
        loads.append(pltpu.make_async_copy(part, target, sems.at[2 + chunks + j]))
    for load in loads:
        load.start()
    for load in loads[: 1 + chunks]:
        load.wait()
    store = pltpu.make_async_copy(x, x_out, sems.at[1])
    store.start()
    halves = 2 if size > HID else 1
    per = len(parts) // halves
    for half in range(halves):
        for load in loads[1 + chunks + half * per : 1 + chunks + (half + 1) * per]:
            load.wait()
        rows = slice(half * per * size, (half + 1) * per * size)
        out[rows, :] = contract(w[rows, :], x[...], 1, 1).astype(BF16)
    store.wait()


def project(place, received, took, parts, name):
    size, count = parts[0].shape[0], len(parts)
    return pl.pallas_call(
        functools.partial(project_kernel, len(took)),
        out_shape=(
            jax.ShapeDtypeStruct((count * size, SUB), BF16),
            jax.ShapeDtypeStruct((SUB, HALF), BF16),
        ),
        in_specs=[SMEM] + [ANY] * (1 + len(took) + count),
        out_specs=(WHOLE, ANY),
        scratch_shapes=[
            pltpu.VMEM((SUB, HALF), BF16),
            pltpu.VMEM((count * size, HALF), BF16),
            pltpu.SemaphoreType.DMA((2 + len(took) + count,)),
        ],
        compiler_params=PARAMS,
        cost_estimate=cost(SHORT),
        name=name,
    )(place, received, *took, *parts)


def block(shape, row=0):
    return pl.BlockSpec(shape, lambda i: (row, 0))


def single(kernel, outs, ins, micros, name):
    return pl.pallas_call(
        kernel,
        grid=(1,),
        out_shape=tuple(jax.ShapeDtypeStruct(shape, kind) for shape, kind in outs),
        in_specs=[block(shape, row) for _, shape, row in ins],
        out_specs=tuple(block(shape) for shape, _ in outs),
        compiler_params=PARAMS,
        cost_estimate=cost(micros),
        name=name,
    )(*[array for array, _, _ in ins])


def full(array):
    return array, array.shape, 0


def hidden_kernel(ours, theirs, dy, active_out, slope_out, hidden_here, *grad_away):
    hidden = [None] * 4
    for j in range(4):
        gate_rows, up_rows = pl.ds(2 * j * HID, HID), pl.ds((2 * j + 1) * HID, HID)
        gate = ours[gate_rows, :].astype(F32) + theirs[gate_rows, :].astype(F32)
        up = ours[up_rows, :].astype(F32) + theirs[up_rows, :].astype(F32)
        sigma = jax.nn.sigmoid(gate)
        active = gate * sigma
        rows = pl.ds(j * HID, HID)
        active_out[rows, :] = active.astype(BF16)
        slope_out[rows, :] = (up * sigma * (1.0 + gate * (1.0 - sigma))).astype(BF16)
        hidden[j] = (active * up).astype(BF16)
    hidden_here[:HID, :] = hidden[0]
    hidden_here[HID:, :] = hidden[1]
    total = contract(jnp.concatenate(hidden[2:], axis=0), dy[...], 1, 0).astype(BF16)
    for j, out in enumerate(grad_away):
        out[...] = total[j * CHUNK : (j + 1) * CHUNK]


def down_here_kernel(rows, x, add0, add1, add2, add3, mine, there):
    mine[...] = contract(rows[:HID, :], x[...], 1, 0)
    mine[:CHUNK, :] += add0[...].astype(F32)
    mine[CHUNK:, :] += add1[...].astype(F32)
    total = contract(rows[HID:, :], x[...], 1, 0)
    there[:CHUNK, :] = (total[:CHUNK] + add2[...].astype(F32)).astype(BF16)
    there[CHUNK:, :] = (total[CHUNK:] + add3[...].astype(F32)).astype(BF16)


def back_kernel(
    place,
    ours,
    theirs,
    active,
    slope,
    x_in,
    part0,
    part1,
    part2,
    part3,
    give0,
    give1,
    keep,
    far0,
    far1,
    far2,
    far3,
    there,
    core,
    mine,
    x,
    w,
    both,
    piece,
    grads,
    own,
    sems,
):
    loads = [pltpu.make_async_copy(x_in, x, sems.at[4])]
    for j, part in enumerate((part0, part1, part2, part3)):
        target = w.at[pl.ds(2 * j * HID, 2 * HID)]
        loads.append(pltpu.make_async_copy(part, target, sems.at[j]))
    for load in loads:
        load.start()
    for j in range(4):
        rows = pl.ds(j * HID, HID)
        grad = ours[rows, :].astype(F32) + theirs[rows, :].astype(F32)
        both[pl.ds(2 * j * HID, HID), :] = (grad * slope[rows, :].astype(F32)).astype(BF16)
        both[pl.ds((2 * j + 1) * HID, HID), :] = (grad * active[rows, :].astype(F32)).astype(BF16)
    stores = []

    def store(source, target):
        copy = pltpu.make_async_copy(source, target, sems.at[5 + len(stores)])
        copy.start()
        stores.append(copy)

    loads[0].wait()
    own[...] = contract(both[: 2 * HID, :], x[...], 1, 0)
    store(own, mine)
    grads[0] = contract(both[6 * HID :, :], x[...], 1, 0).astype(BF16)
    for j, target in enumerate((far0, far1, far2, far3)):
        store(grads.at[0, pl.ds(j * CHUNK, CHUNK)], target)
    for slot, target in ((1, there), (2, core)):
        rows = slice(slot * 2 * HID, (slot + 1) * 2 * HID)
        grads[slot] = contract(both[rows, :], x[...], 1, 0).astype(BF16)
        store(grads.at[slot], target)
    for load in loads[1:]:
        load.wait()
    piece[1] = contract(both[...], w[:, columns(place, False)], 0, 0).astype(BF16)
    store(piece.at[1], keep.at[pl.ds(0, SUB)])
    for part, target in enumerate((give0, give1)):
        rows = slice(part * CUT, (part + 1) * CUT)
        piece[0, rows, :] = contract(both[:, rows], w[:, columns(place, True)], 0, 0).astype(BF16)
        store(piece.at[0, pl.ds(part * CUT, CUT)], target)
    for copy in stores:
        copy.wait()


def back_products(place, ours, theirs, active, slope, x, parts):
    outs = [((CUT, QUARTER), BF16)] * 2 + [((ROWS, QUARTER), BF16)]
    outs += [((CHUNK, HALF), BF16)] * 4 + [((2 * HID, HALF), BF16)] * 2 + [((2 * HID, HALF), F32)]
    return pl.pallas_call(
        back_kernel,
        grid=(1,),
        out_shape=tuple(jax.ShapeDtypeStruct(shape, kind) for shape, kind in outs),
        in_specs=[SMEM] + [block((4 * HID, SUB))] * 4 + [ANY] * 5,
        out_specs=(ANY,) * 10,
        scratch_shapes=[
            pltpu.VMEM((SUB, HALF), BF16),
            pltpu.VMEM((8 * HID, HALF), BF16),
            pltpu.VMEM((8 * HID, SUB), BF16),
            pltpu.VMEM((2, SUB, QUARTER), BF16),
            pltpu.VMEM((3, 2 * HID, HALF), BF16),
            pltpu.VMEM((2 * HID, HALF), F32),
            pltpu.SemaphoreType.DMA((15,)),
        ],
        compiler_params=PARAMS,
        cost_estimate=cost(SHORT),
        name="back_products",
    )(place, ours, theirs, active, slope, x, *parts)


def adam_kernel(terms, weight, first, second, *refs):
    new_weight, new_first, new_second = refs[-3:]
    grad = refs[0][...].astype(F32)
    for term in refs[1:terms]:
        grad += term[...].astype(F32)
    new_weight[...], new_first[...], new_second[...] = adam_step(
        weight[...], first[...], second[...], grad
    )


def adam(weight, first, second, terms, took, name, flops=1):
    step = 32
    flat = (took.shape[0], HALF)
    spec = pl.BlockSpec((step, HALF), lambda i: (i, 0))
    return pl.pallas_call(
        functools.partial(adam_kernel, len(terms) + 1),
        grid=(flat[0] // step,),
        out_shape=(
            jax.ShapeDtypeStruct(flat, BF16),
            jax.ShapeDtypeStruct(flat, F32),
            jax.ShapeDtypeStruct(flat, F32),
        ),
        in_specs=[spec] * (4 + len(terms)),
        out_specs=(spec,) * 3,
        compiler_params=pltpu.CompilerParams(vmem_limit_bytes=16 * 1024 * 1024),
        cost_estimate=pl.CostEstimate(flops=flops, bytes_accessed=1, transcendentals=0),
        name=name,
    )(weight.reshape(flat), first.reshape(flat), second.reshape(flat), *terms, took)


def per_device(
    tokens,
    out_grad,
    expert_ids,
    route_weights,
    gate_up_weight,
    down_weight,
    gate_up_m,
    gate_up_v,
    down_m,
    down_v,
):
    ep = lax.axis_index("ep")
    rep = lax.axis_index("rep")
    y_hi = rep // 2
    core = rep % 2
    place = jnp.stack([ep // 16, y_hi, core]).astype(jnp.int32)
    ids_t = expert_ids.T
    weight_t = route_weights.T

    own_gu, own_down = gate_up_weight.reshape(2 * HID, HALF), down_weight.reshape(HID, HALF)
    y_gu, y_down = from_partner(own_gu, "rep", 2), from_partner(own_down, "rep", 2)
    core_gu, core_down = from_partner(own_gu, "rep", 1), from_partner(own_down, "rep", 1)
    far_gu, far_down = from_partner(y_gu, "rep", 1), from_partner(y_down, "rep", 1)

    send_x, pick = send(
        send_tokens_kernel, place, [ids_t], tokens, [(ROWS, QUARTER), (ROWS, 2 * TOK)], "send_tokens"
    )
    got_x = exchange(send_x)
    took_x = from_partner(got_x[SUB:], "rep", 1)
    (send_dy,) = send(
        send_grads_kernel, place, [ids_t, weight_t, pick], out_grad, [(ROWS, QUARTER)], "send_grads"
    )
    send_dy, far_gu = lax.optimization_barrier((send_dy, far_gu))
    got_dy = exchange(send_dy)

    gu_parts = (own_gu, y_gu, core_gu, far_gu)
    part_gu, row_x = project(place, got_x, [took_x], gu_parts, "project_gate_up")
    there_gu = from_partner(part_gu, "ep", 1)
    late_dy, _ = lax.optimization_barrier((got_dy, part_gu))
    took_dy = from_partner(late_dy[SUB:], "rep", 1)
    part_hg, row_dy = project(
        place, late_dy, [took_dy], (own_down, y_down, core_down, far_down), "project_down"
    )
    there_hg = from_partner(part_hg, "ep", 1)

    half = (2 * HID, SUB)
    active, slope, hidden_here, *down_away = single(
        hidden_kernel,
        [((4 * HID, SUB), BF16), ((4 * HID, SUB), BF16), (half, BF16)]
        + [((CHUNK, HALF), BF16)] * 4,
        [full(part_gu), full(there_gu), full(row_dy)],
        SHORT,
        "hidden_and_down",
    )
    down_mine, down_send = single(
        down_here_kernel,
        [((HID, HALF), F32), ((HID, HALF), BF16)],
        [full(hidden_here), full(row_dy)]
        + [full(from_partner(chunk, "rep", 1)) for chunk in down_away],
        SHORT,
        "down_here",
    )
    active, slope, down_send = lax.optimization_barrier((active, slope, down_send))
    down_there = from_partner(down_send, "rep", 2)
    give0, give1, keep, *far, there, toward_core, mine = back_products(
        place, part_hg, there_hg, active, slope, row_x, gu_parts
    )
    took_far = [from_partner(chunk, "rep", 1) for chunk in far]
    send_there = (there.astype(F32) + jnp.concatenate(took_far).astype(F32)).astype(BF16)
    gu_there = from_partner(send_there, "rep", 2)
    took_give = [from_partner(chunk, "rep", 1) for chunk in (give0, give1)]
    took_give, down_there = lax.optimization_barrier((took_give, down_there))
    for j, chunk in enumerate(took_give):
        keep = lax.dynamic_update_slice(keep, chunk, (SUB + j * CUT, 0))
    toward_core, keep = lax.optimization_barrier((toward_core, keep))
    back = exchange(keep)
    mine = mine + from_partner(toward_core, "rep", 1).astype(F32)
    new_down, down_first, down_second = adam(
        down_weight, down_m, down_v, (down_mine,), down_there, "adam_down"
    )
    new_gu, gu_first, gu_second = adam(
        gate_up_weight, gate_up_m, gate_up_v, (mine,), gu_there, "adam_gate_up", UPDATE
    )
    back, new_gu = lax.optimization_barrier((back, new_gu))
    token_sum = contract(pick, back, 0, 0)
    lower, upper = token_sum[:TOK], token_sum[TOK:]
    keep_sum = jnp.where(y_hi == 0, lower, upper)
    give_sum = jnp.where(y_hi == 0, upper, lower).astype(BF16)
    took_sum, new_down = lax.optimization_barrier((from_partner(give_sum, "rep", 2), new_down))
    token_grad = (keep_sum + took_sum.astype(F32)).astype(BF16)
    gu, down = gate_up_weight.shape, down_weight.shape
    return (
        token_grad,
        new_gu.reshape(gu),
        new_down.reshape(down),
        gu_first.reshape(gu),
        gu_second.reshape(gu),
        down_first.reshape(down),
        down_second.reshape(down),
    )


def solution(mesh):
    in_specs = (
        P("ep", None),
        P("ep", None),
        P("ep", None),
        P("ep", None),
        P("ep", None, "rep", None),
        P("ep", "rep", None),
        P("ep", None, "rep", None),
        P("ep", None, "rep", None),
        P("ep", "rep", None),
        P("ep", "rep", None),
    )
    out_specs = (
        P("ep", "rep"),
        P("ep", None, "rep", None),
        P("ep", "rep", None),
        P("ep", None, "rep", None),
        P("ep", None, "rep", None),
        P("ep", "rep", None),
        P("ep", "rep", None),
    )
    return jax.shard_map(
        per_device, mesh=mesh, in_specs=in_specs, out_specs=out_specs, check_vma=False
    )
```

```python
import functools

import jax
import jax.numpy as jnp
from jax import lax
from jax.experimental import pallas as pl
from jax.experimental.pallas import tpu as pltpu
from jax.sharding import PartitionSpec as P

beta_first = 0.9
beta_second = 0.95
learn_rate = 0.01
decay_rate = 0.1
adam_epsilon = 1e-08
correct_first = 0.9999734386011124
correct_second = 0.994079470779666

N_EP = 32
EXPERTS = 16
TOK = 128
TOP = 8
HALF_ROWS = 40
ROWS = N_EP * HALF_ROWS
QUARTER = 1024
HALF = 2048
HID = 192
F32 = jnp.float32
SCALE = 1_000_000
UPDATE = 5 * 10**12
BF16 = jnp.bfloat16


SHORT = 0.03


def cost(micros):
    return pl.CostEstimate(flops=1, bytes_accessed=int(micros * SCALE), transcendentals=0)


def from_partner(value, axis, mask):
    pairs = [(source, source ^ mask) for source in range(lax.axis_size(axis))]
    return lax.ppermute(value, axis, pairs)


def exchange_groups():
    groups = []
    for core in range(2):
        for plane in range(2):
            members = []
            for step in range(N_EP):
                ep = (step + 16 * core) % N_EP
                y_hi = plane ^ (ep // 16) if core == 1 else plane
                members.append(ep * 4 + y_hi * 2 + core)
            groups.append(members)
    return groups


def exchange(value):
    return lax.all_to_all(
        value.reshape(N_EP, HALF_ROWS, QUARTER),
        ("ep", "rep"),
        split_axis=0,
        concat_axis=0,
        tiled=True,
        axis_index_groups=exchange_groups(),
    ).reshape(ROWS, QUARTER)


def contract(left, right, left_dim, right_dim):
    return lax.dot_general(
        left, right, (((left_dim,), (right_dim,)), ((), ())), preferred_element_type=F32
    )


def adam_step(weight, first, second, grad):
    first_new = beta_first * first + (1.0 - beta_first) * grad
    second_new = beta_second * second + (1.0 - beta_second) * grad * grad
    wide = weight.astype(F32)
    update = first_new / correct_first / (jnp.sqrt(second_new / correct_second) + adam_epsilon)
    return (
        (wide - learn_rate * (update + decay_rate * wide)).astype(BF16),
        first_new,
        second_new,
    )


def slot_match(place, ids_t):
    y_lo, y_hi, core = place[0], place[1], place[2]
    expert = lax.broadcasted_iota(jnp.int32, (EXPERTS, TOK), 0)
    named = jnp.zeros((EXPERTS, TOK), jnp.int32)
    for k in range(TOP):
        named += jnp.where(ids_t[k : k + 1, :] == expert, 1, 0)
    earlier = (
        lax.broadcasted_iota(jnp.int32, (TOK, TOK), 0)
        < lax.broadcasted_iota(jnp.int32, (TOK, TOK), 1)
    ).astype(F32)
    rank = contract(named.astype(F32).astype(BF16), earlier.astype(BF16), 1, 0)
    code = jnp.where(named > 0, rank, -1.0).astype(BF16)
    turn = core * (ROWS // 2)
    row = lax.broadcasted_iota(jnp.int32, (ROWS, EXPERTS), 0) + turn
    row = jnp.where(row >= ROWS, row - ROWS, row)
    low = lax.broadcasted_iota(jnp.int32, (ROWS, EXPERTS), 1) * (2 * HALF_ROWS)
    spread = jnp.where((row >= low) & (row < low + 2 * HALF_ROWS), 1.0, 0.0).astype(BF16)
    code_row = contract(spread, code, 1, 0)
    line = lax.broadcasted_iota(jnp.int32, (ROWS, TOK), 0) + turn
    line = jnp.where(line >= ROWS, line - ROWS, line)
    block = (line * 1639) >> 16
    flip = jnp.where(core == 1, 1, 0)
    half = y_hi ^ (flip & (y_lo ^ (block >> 4)))
    wanted = line - block * HALF_ROWS + half * HALF_ROWS
    match = code_row == wanted.astype(F32)
    return match, block & 1, spread


def pick_matrix(match, holder):
    low = jnp.where(match & (holder == 0), 1.0, 0.0)
    high = jnp.where(match & (holder == 1), 1.0, 0.0)
    return jnp.concatenate([low, high], axis=1).astype(BF16)


def send_tokens_kernel(place, ids_ref, low, high, out, pick_ref):
    match, holder, _ = slot_match(place, ids_ref[...])
    pick = pick_matrix(match, holder)
    pick_ref[...] = pick
    out[...] = (
        contract(pick[:, :TOK], low[...], 1, 0) + contract(pick[:, TOK:], high[...], 1, 0)
    ).astype(BF16)


def send_grads_kernel(place, ids_ref, weight_ref, pick_ref, low, high, out):
    ids = ids_ref[...]
    match, _, spread = slot_match(place, ids)
    expert = lax.broadcasted_iota(jnp.int32, (EXPERTS, TOK), 0)
    weight = weight_ref[...]
    coeff = jnp.zeros((EXPERTS, TOK), F32)
    for k in range(TOP):
        coeff += jnp.where(ids[k : k + 1, :] == expert, weight[k : k + 1, :], 0.0)
    first = coeff.astype(BF16)
    rest = coeff - first.astype(F32)
    second = rest.astype(BF16)
    third = (rest - second.astype(F32)).astype(BF16)
    wide = (contract(spread, first, 1, 0) + contract(spread, second, 1, 0)) + contract(
        spread, third, 1, 0
    )
    scale = jnp.sum(jnp.where(match, wide, 0.0), axis=1, keepdims=True)
    rows = contract(pick_ref[:, :TOK], low[...], 1, 0) + contract(
        pick_ref[:, TOK:], high[...], 1, 0
    )
    out[...] = (scale * rows).astype(BF16)


def quarter_spec(first):
    return pl.BlockSpec((TOK, QUARTER), lambda i, place: (0, first + place[2]))


def fixed_spec(shape):
    return pl.BlockSpec(shape, lambda i, place: (0, 0))


def send(kernel, place, small, wide, outs, name):
    specs = [fixed_spec(array.shape) for array in small]
    return pl.pallas_call(
        kernel,
        out_shape=tuple(jax.ShapeDtypeStruct(shape, BF16) for shape in outs),
        grid_spec=pltpu.PrefetchScalarGridSpec(
            num_scalar_prefetch=1,
            grid=(1,),
            in_specs=specs + [quarter_spec(0), quarter_spec(2)],
            out_specs=tuple(fixed_spec(shape) for shape in outs),
        ),
        compiler_params=pltpu.CompilerParams(vmem_limit_bytes=48 * 1024 * 1024),
        cost_estimate=cost(3),
        name=name,
    )(place, *small, wide, wide)


SUB = ROWS // 2
CHUNK = HID // 2
CUT = SUB // 2
ANY = pl.BlockSpec(memory_space=pl.ANY)
WHOLE = pl.BlockSpec(memory_space=pltpu.VMEM)
SMEM = pl.BlockSpec(memory_space=pltpu.SMEM)
PARAMS = pltpu.CompilerParams(vmem_limit_bytes=56 * 1024 * 1024)


def columns(place, other):
    start = pl.multiple_of(jnp.where(other, 1 - place[2], place[2]) * QUARTER, QUARTER)
    return pl.ds(start, QUARTER)


def project_kernel(chunks, place, own, *refs):
    took, refs = refs[:chunks], refs[chunks:]
    parts, (out, x_out, x, w, sems) = refs[:-5], refs[-5:]
    size, step = parts[0].shape[0], SUB // chunks
    loads = [
        pltpu.make_async_copy(own.at[pl.ds(0, SUB)], x.at[:, columns(place, False)], sems.at[0])
    ]
    for j, chunk in enumerate(took):
        target = x.at[pl.ds(j * step, step), columns(place, True)]
        loads.append(pltpu.make_async_copy(chunk, target, sems.at[2 + j]))
    for j, part in enumerate(parts):
        target = w.at[pl.ds(j * size, size)]
        loads.append(pltpu.make_async_copy(part, target, sems.at[2 + chunks + j]))
    for load in loads:
        load.start()
    for load in loads[: 1 + chunks]:
        load.wait()
    store = pltpu.make_async_copy(x, x_out, sems.at[1])
    store.start()
    halves = 2 if size > HID else 1
    per = len(parts) // halves
    for half in range(halves):
        for load in loads[1 + chunks + half * per : 1 + chunks + (half + 1) * per]:
            load.wait()
        rows = slice(half * per * size, (half + 1) * per * size)
        out[rows, :] = contract(w[rows, :], x[...], 1, 1).astype(BF16)
    store.wait()


def project(place, received, took, parts, name):
    size, count = parts[0].shape[0], len(parts)
    return pl.pallas_call(
        functools.partial(project_kernel, len(took)),
        out_shape=(
            jax.ShapeDtypeStruct((count * size, SUB), BF16),
            jax.ShapeDtypeStruct((SUB, HALF), BF16),
        ),
        in_specs=[SMEM] + [ANY] * (1 + len(took) + count),
        out_specs=(WHOLE, ANY),
        scratch_shapes=[
            pltpu.VMEM((SUB, HALF), BF16),
            pltpu.VMEM((count * size, HALF), BF16),
            pltpu.SemaphoreType.DMA((2 + len(took) + count,)),
        ],
        compiler_params=PARAMS,
        cost_estimate=cost(SHORT),
        name=name,
    )(place, received, *took, *parts)


def block(shape, row=0):
    return pl.BlockSpec(shape, lambda i: (row, 0))


def single(kernel, outs, ins, micros, name):
    return pl.pallas_call(
        kernel,
        grid=(1,),
        out_shape=tuple(jax.ShapeDtypeStruct(shape, kind) for shape, kind in outs),
        in_specs=[block(shape, row) for _, shape, row in ins],
        out_specs=tuple(block(shape) for shape, _ in outs),
        compiler_params=PARAMS,
        cost_estimate=cost(micros),
        name=name,
    )(*[array for array, _, _ in ins])


def full(array):
    return array, array.shape, 0


def hidden_kernel(ours, theirs, dy, active_out, slope_out, hidden_here, *grad_away):
    hidden = [None] * 4
    for j in range(4):
        gate_rows, up_rows = pl.ds(2 * j * HID, HID), pl.ds((2 * j + 1) * HID, HID)
        gate = ours[gate_rows, :].astype(F32) + theirs[gate_rows, :].astype(F32)
        up = ours[up_rows, :].astype(F32) + theirs[up_rows, :].astype(F32)
        sigma = jax.nn.sigmoid(gate)
        active = gate * sigma
        rows = pl.ds(j * HID, HID)
        active_out[rows, :] = active.astype(BF16)
        slope_out[rows, :] = (up * sigma * (1.0 + gate * (1.0 - sigma))).astype(BF16)
        hidden[j] = (active * up).astype(BF16)
    hidden_here[:HID, :] = hidden[0]
    hidden_here[HID:, :] = hidden[1]
    total = contract(jnp.concatenate(hidden[2:], axis=0), dy[...], 1, 0).astype(BF16)
    for j, out in enumerate(grad_away):
        out[...] = total[j * CHUNK : (j + 1) * CHUNK]


def down_here_kernel(rows, x, add0, add1, add2, add3, mine, there):
    mine[...] = contract(rows[:HID, :], x[...], 1, 0)
    mine[:CHUNK, :] += add0[...].astype(F32)
    mine[CHUNK:, :] += add1[...].astype(F32)
    total = contract(rows[HID:, :], x[...], 1, 0)
    there[:CHUNK, :] = (total[:CHUNK] + add2[...].astype(F32)).astype(BF16)
    there[CHUNK:, :] = (total[CHUNK:] + add3[...].astype(F32)).astype(BF16)


def back_kernel(
    place,
    ours,
    theirs,
    active,
    slope,
    x_in,
    part0,
    part1,
    part2,
    part3,
    give0,
    give1,
    keep,
    far0,
    far1,
    far2,
    far3,
    there,
    core,
    mine,
    x,
    w,
    both,
    piece,
    grads,
    own,
    sems,
):
    loads = [pltpu.make_async_copy(x_in, x, sems.at[4])]
    for j, part in enumerate((part0, part1, part2, part3)):
        target = w.at[pl.ds(2 * j * HID, 2 * HID)]
        loads.append(pltpu.make_async_copy(part, target, sems.at[j]))
    for load in loads:
        load.start()
    for j in range(4):
        rows = pl.ds(j * HID, HID)
        grad = ours[rows, :].astype(F32) + theirs[rows, :].astype(F32)
        both[pl.ds(2 * j * HID, HID), :] = (grad * slope[rows, :].astype(F32)).astype(BF16)
        both[pl.ds((2 * j + 1) * HID, HID), :] = (grad * active[rows, :].astype(F32)).astype(BF16)
    stores = []

    def store(source, target):
        copy = pltpu.make_async_copy(source, target, sems.at[5 + len(stores)])
        copy.start()
        stores.append(copy)

    loads[0].wait()
    own[...] = contract(both[: 2 * HID, :], x[...], 1, 0).astype(BF16)
    store(own, mine)
    grads[0] = contract(both[6 * HID :, :], x[...], 1, 0).astype(BF16)
    for j, target in enumerate((far0, far1, far2, far3)):
        store(grads.at[0, pl.ds(j * CHUNK, CHUNK)], target)
    for slot, target in ((1, there), (2, core)):
        rows = slice(slot * 2 * HID, (slot + 1) * 2 * HID)
        grads[slot] = contract(both[rows, :], x[...], 1, 0).astype(BF16)
        store(grads.at[slot], target)
    for load in loads[1:]:
        load.wait()
    piece[1] = contract(both[...], w[:, columns(place, False)], 0, 0).astype(BF16)
    store(piece.at[1], keep.at[pl.ds(0, SUB)])
    for part, target in enumerate((give0, give1)):
        rows = slice(part * CUT, (part + 1) * CUT)
        piece[0, rows, :] = contract(both[:, rows], w[:, columns(place, True)], 0, 0).astype(BF16)
        store(piece.at[0, pl.ds(part * CUT, CUT)], target)
    for copy in stores:
        copy.wait()


def back_products(place, ours, theirs, active, slope, x, parts):
    outs = [((CUT, QUARTER), BF16)] * 2 + [((ROWS, QUARTER), BF16)]
    outs += [((CHUNK, HALF), BF16)] * 4 + [((2 * HID, HALF), BF16)] * 3
    return pl.pallas_call(
        back_kernel,
        grid=(1,),
        out_shape=tuple(jax.ShapeDtypeStruct(shape, kind) for shape, kind in outs),
        in_specs=[SMEM] + [block((4 * HID, SUB))] * 4 + [ANY] * 5,
        out_specs=(ANY,) * 10,
        scratch_shapes=[
            pltpu.VMEM((SUB, HALF), BF16),
            pltpu.VMEM((8 * HID, HALF), BF16),
            pltpu.VMEM((8 * HID, SUB), BF16),
            pltpu.VMEM((2, SUB, QUARTER), BF16),
            pltpu.VMEM((3, 2 * HID, HALF), BF16),
            pltpu.VMEM((2 * HID, HALF), BF16),
            pltpu.SemaphoreType.DMA((15,)),
        ],
        compiler_params=PARAMS,
        cost_estimate=cost(SHORT),
        name="back_products",
    )(place, ours, theirs, active, slope, x, *parts)


def adam_kernel(terms, weight, first, second, *refs):
    new_weight, new_first, new_second = refs[-3:]
    grad = refs[0][...].astype(F32)
    for term in refs[1:terms]:
        grad += term[...].astype(F32)
    new_weight[...], new_first[...], new_second[...] = adam_step(
        weight[...], first[...], second[...], grad
    )


def adam(weight, first, second, terms, took, name, flops=1):
    step = 64
    flat = (took.shape[0], HALF)
    spec = pl.BlockSpec((step, HALF), lambda i: (i, 0))
    return pl.pallas_call(
        functools.partial(adam_kernel, len(terms) + 1),
        grid=(flat[0] // step,),
        out_shape=(
            jax.ShapeDtypeStruct(flat, BF16),
            jax.ShapeDtypeStruct(flat, F32),
            jax.ShapeDtypeStruct(flat, F32),
        ),
        in_specs=[spec] * (4 + len(terms)),
        out_specs=(spec,) * 3,
        compiler_params=pltpu.CompilerParams(vmem_limit_bytes=16 * 1024 * 1024),
        cost_estimate=pl.CostEstimate(flops=flops, bytes_accessed=1, transcendentals=0),
        name=name,
    )(weight.reshape(flat), first.reshape(flat), second.reshape(flat), *terms, took)


def per_device(
    tokens,
    out_grad,
    expert_ids,
    route_weights,
    gate_up_weight,
    down_weight,
    gate_up_m,
    gate_up_v,
    down_m,
    down_v,
):
    ep = lax.axis_index("ep")
    rep = lax.axis_index("rep")
    y_hi = rep // 2
    core = rep % 2
    place = jnp.stack([ep // 16, y_hi, core]).astype(jnp.int32)
    ids_t = expert_ids.T
    weight_t = route_weights.T

    own_gu, own_down = gate_up_weight.reshape(2 * HID, HALF), down_weight.reshape(HID, HALF)
    y_gu, y_down = from_partner(own_gu, "rep", 2), from_partner(own_down, "rep", 2)
    core_gu, core_down = from_partner(own_gu, "rep", 1), from_partner(own_down, "rep", 1)
    far_gu, far_down = from_partner(y_gu, "rep", 1), from_partner(y_down, "rep", 1)

    send_x, pick = send(
        send_tokens_kernel, place, [ids_t], tokens, [(ROWS, QUARTER), (ROWS, 2 * TOK)], "send_tokens"
    )
    got_x = exchange(send_x)
    took_x = from_partner(got_x[SUB:], "rep", 1)
    (send_dy,) = send(
        send_grads_kernel, place, [ids_t, weight_t, pick], out_grad, [(ROWS, QUARTER)], "send_grads"
    )
    send_dy, far_gu = lax.optimization_barrier((send_dy, far_gu))
    got_dy = exchange(send_dy)

    gu_parts = (own_gu, y_gu, core_gu, far_gu)
    part_gu, row_x = project(place, got_x, [took_x], gu_parts, "project_gate_up")
    there_gu = from_partner(part_gu, "ep", 1)
    late_dy, _ = lax.optimization_barrier((got_dy, part_gu))
    took_dy = from_partner(late_dy[SUB:], "rep", 1)
    part_hg, row_dy = project(
        place, late_dy, [took_dy], (own_down, y_down, core_down, far_down), "project_down"
    )
    there_hg = from_partner(part_hg, "ep", 1)

    half = (2 * HID, SUB)
    active, slope, hidden_here, *down_away = single(
        hidden_kernel,
        [((4 * HID, SUB), BF16), ((4 * HID, SUB), BF16), (half, BF16)]
        + [((CHUNK, HALF), BF16)] * 4,
        [full(part_gu), full(there_gu), full(row_dy)],
        SHORT,
        "hidden_and_down",
    )
    down_mine, down_send = single(
        down_here_kernel,
        [((HID, HALF), F32), ((HID, HALF), BF16)],
        [full(hidden_here), full(row_dy)]
        + [full(from_partner(chunk, "rep", 1)) for chunk in down_away],
        SHORT,
        "down_here",
    )
    active, slope, down_send = lax.optimization_barrier((active, slope, down_send))
    down_there = from_partner(down_send, "rep", 2)
    give0, give1, keep, *far, there, toward_core, mine = back_products(
        place, part_hg, there_hg, active, slope, row_x, gu_parts
    )
    took_far = [from_partner(chunk, "rep", 1) for chunk in far]
    send_there = (there.astype(F32) + jnp.concatenate(took_far).astype(F32)).astype(BF16)
    gu_there = from_partner(send_there, "rep", 2)
    took_give = [from_partner(chunk, "rep", 1) for chunk in (give0, give1)]
    took_give, down_there = lax.optimization_barrier((took_give, down_there))
    for j, chunk in enumerate(took_give):
        keep = lax.dynamic_update_slice(keep, chunk, (SUB + j * CUT, 0))
    toward_core, keep = lax.optimization_barrier((toward_core, keep))
    back = exchange(keep)
    mine = mine.astype(F32) + from_partner(toward_core, "rep", 1).astype(F32)
    new_down, down_first, down_second = adam(
        down_weight, down_m, down_v, (down_mine,), down_there, "adam_down"
    )
    new_gu, gu_first, gu_second = adam(
        gate_up_weight, gate_up_m, gate_up_v, (mine,), gu_there, "adam_gate_up", UPDATE
    )
    back, new_gu = lax.optimization_barrier((back, new_gu))
    token_sum = contract(pick, back, 0, 0)
    lower, upper = token_sum[:TOK], token_sum[TOK:]
    keep_sum = jnp.where(y_hi == 0, lower, upper)
    give_sum = jnp.where(y_hi == 0, upper, lower).astype(BF16)
    took_sum, new_down = lax.optimization_barrier((from_partner(give_sum, "rep", 2), new_down))
    token_grad = (keep_sum + took_sum.astype(F32)).astype(BF16)
    gu, down = gate_up_weight.shape, down_weight.shape
    return (
        token_grad,
        new_gu.reshape(gu),
        new_down.reshape(down),
        gu_first.reshape(gu),
        gu_second.reshape(gu),
        down_first.reshape(down),
        down_second.reshape(down),
    )


def solution(mesh):
    in_specs = (
        P("ep", None),
        P("ep", None),
        P("ep", None),
        P("ep", None),
        P("ep", None, "rep", None),
        P("ep", "rep", None),
        P("ep", None, "rep", None),
        P("ep", None, "rep", None),
        P("ep", "rep", None),
        P("ep", "rep", None),
    )
    out_specs = (
        P("ep", "rep"),
        P("ep", None, "rep", None),
        P("ep", "rep", None),
        P("ep", None, "rep", None),
        P("ep", None, "rep", None),
        P("ep", "rep", None),
        P("ep", "rep", None),
    )
    return jax.shard_map(
        per_device, mesh=mesh, in_specs=in_specs, out_specs=out_specs, check_vma=False
    )
```
